32 devices in a mesh: parts: 2 (over y), cluster: 4 (over z), tensor: 4 (over x, core).
Axes of the slice: x: 2, y: 2, z: 4, core: 2. Of those that a mesh axis runs over, the one named last changes fastest.
Arguments:
- hidden_rows: bfloat16 [128, 4096], P(('parts', 'cluster', 'tensor')), parts along dimension 0, may hold values from -5 to 5
- expert_ids: int32 [128, 2], P(('parts', 'cluster', 'tensor')), parts along dimension 0, may hold values from 0 to 3, all different within a row; in each aligned block of 4 rows (0 to 3, 4 to 7, ...) at most 2 rows name the same one
- weight_codes: int32 [128, 2], P(('parts', 'cluster', 'tensor')), parts along dimension 0, may hold values from 1 to 64
- target_rows: int32 [128], P(('parts', 'cluster', 'tensor')), parts along dimension 0, may hold values from 0 to 3, as said below
- norm_gain: float32 [4, 4096], replicated, may hold values from 0.5 to 1.5
- norm_bias: float32 [4, 4096], replicated, may hold values from -3 to 3
- head_weight: bfloat16 [4096, 131072], P(None, ('cluster', 'tensor')), may hold values from -1 to 1
Outputs:
- next_logprob: float32 [128, 32768], P(('parts', 'cluster', 'tensor')), parts along dimension 0
The draws below stay inside these ranges and needn't reach their ends.
There are 2 independent parts, one for each index of `parts`. The reference program is written for one: setup_inputs(seed, part) draws one part's arguments, and reference() takes and returns one part's arrays. A program takes and returns all parts, laid end to end along the dimension named above; an argument that names none is the same for every part. Nothing has to cross between parts.
Inputs may be any that keep to these rules, and one draw needn't show every extreme that they name: `expert_ids`: A request's 2 ids differ. Among the 4 requests of one device no expert is named more than 2 times, and in some such block one expert is named exactly 2 times. `target_rows`: in each aligned block of 4 requests the entries are a permutation of 0 to 3.
All inputs are finite; a program needn't handle non-finite values.
Results may differ from the reference program's by a relative error of at most 0.0009.
Values may be sent and summed in bfloat16 or wider, within the bound.
A program may use at most 192 MiB of HBM per device.

```python
import math
import jax
import jax.numpy as jnp
import numpy as np
from jax import lax

D = 4096
VOCAB = 32768
EXPERTS = 4
TOPK = 2
REQ_DEV = 4
MOST = 2
REQ = 64


def draw_hidden_rows(key, part):
    key = jax.random.fold_in(key, 11)
    third = jax.random.fold_in(key, 2)
    values = jnp.clip(jax.random.normal(third, (REQ, D), jnp.float32), -5.0, 5.0)
    return values.astype(jnp.bfloat16)


def draw_target_rows(key, part):
    key = jax.random.fold_in(key, 31)
    keys = jax.random.split(key, REQ // REQ_DEV)
    blocks = jax.vmap(lambda single: jax.random.permutation(single, REQ_DEV))(keys)
    return blocks.reshape(REQ).astype(jnp.int32)


def draw_head_weight(key, part):
    key = jax.random.fold_in(key, 23)
    first, second = jax.random.split(key, 2)
    columns = EXPERTS * VOCAB
    position = (jnp.arange(columns) % VOCAB).astype(jnp.float32) / VOCAB
    spread = jnp.exp(jax.random.uniform(first, (columns,), jnp.float32, 0.0, math.log(10.0)))
    scale = 0.5 * (1.0 + 2.0 * position) * spread / math.sqrt(D)
    values = jnp.clip(jax.random.normal(second, (D, columns), jnp.float32), -4.0, 4.0) * scale[None, :]
    return values.astype(jnp.bfloat16)


def place_ends(drawn, stream_key, smallest, largest):
    place = [jax.random.randint(jax.random.fold_in(stream_key, axis), (), 0, length) for axis, length in enumerate(drawn.shape)]
    widest = drawn.shape.index(max(drawn.shape))
    neighbour = place[:widest] + [(place[widest] + 1) % drawn.shape[widest]] + place[widest + 1:]
    return drawn.at[tuple(place)].set(smallest).at[tuple(neighbour)].set(largest)


def deal_out(key, own, number, rows, number_of, top, reach, skew):
    ranking = jax.random.permutation(key, number_of)
    crowded, common = shares(number_of, rows * top, reach, skew, True), shares(number_of, rows * top, reach, skew, False)
    places = jnp.arange(number_of)

    def named(lengths, turn):
        used = int((lengths > 0).sum())
        fixed = max(1, used // 4)
        moved = fixed + (places - fixed + turn * (used - fixed)) % max(1, number_of - fixed)
        return jnp.zeros((number_of,), jnp.int32).at[ranking[jnp.where(places < fixed, places, moved)]].set(jnp.asarray(lengths, jnp.int32))

    lengths = jnp.where(number % 4 == 0, named(crowded, number // 4), named(common, number - number // 4 - 1))
    mixed = jax.random.permutation(jax.random.fold_in(own, 3), number_of)
    source_of, taker = mixed[0:number_of // 2 * 2:2], mixed[1:number_of // 2 * 2:2]
    slack = jnp.minimum(lengths[source_of] - 1, reach - lengths[taker]) // 2
    slack = jnp.where((source_of == ranking[0]) | (taker == ranking[0]) | (lengths[taker] == 0), 0, jnp.maximum(slack, 0))
    moved = jax.random.randint(jax.random.fold_in(own, 4), (number_of // 2,), 0, 1 << 20) % (slack + 1)
    lengths = lengths.at[source_of].add(-moved).at[taker].add(moved)
    members = jnp.searchsorted(jnp.cumsum(lengths), jnp.arange(rows * top), side="right").astype(jnp.int32)
    table = members.reshape(top, rows).T
    table = table[jax.random.permutation(jax.random.fold_in(own, 1), rows)]
    turn = jax.random.randint(jax.random.fold_in(own, 2), (rows, 1), 0, top)
    return jnp.take_along_axis(table, (jnp.arange(top)[None, :] + turn) % top, axis=1)


def shares(count, total, most, skew, full):
    loads = [(1 << 20) // math.isqrt(grade ** skew) + 1 for grade in range(1, count + 1)]
    largest = most if full else min(most, max(-(-total // count), total * loads[0] // sum(loads)))
    least = 1 if total - largest >= count - 1 else 0
    counts, spare = [largest] + [least] * (count - 1), total - largest - least * (count - 1)
    while spare > 0:
        candidates = [i for i in range(1, count) if counts[i] < largest] or [i for i in range(1, count) if counts[i] < most]
        whole, left = sum([loads[i] for i in candidates]), spare
        for i in candidates:
            addition = min(most - counts[i], max(1, left * loads[i] // whole), spare)
            counts[i] = counts[i] + addition
            spare = spare - addition
    return np.array(counts)


def gaussian(rng, shape, width, most, held_as=jnp.bfloat16):
    return jnp.clip(width * jax.random.normal(rng, shape, jnp.float32), -most, most).astype(held_as)


def setup_inputs(seed: int = 0, part: int = 0) -> dict:
    streams_of = jax.random.split(jax.random.key(seed), 8)
    part_keys = jax.random.split(jax.random.fold_in(streams_of[7], part), 8)
    hidden_rows = draw_hidden_rows(jax.random.fold_in(jax.random.fold_in(streams_of[7], part), 71), part)
    expert_ids_keys = jax.random.split(jax.random.fold_in(part_keys[1], 1), REQ // REQ_DEV)
    expert_ids_turns = jax.random.permutation(jax.random.fold_in(part_keys[1], 3), REQ // REQ_DEV)
    expert_ids = jax.vmap(lambda own, number: deal_out(jax.random.fold_in(part_keys[1], 2), own, number, REQ_DEV, EXPERTS, TOPK, MOST, 2))(expert_ids_keys, expert_ids_turns).reshape((REQ, TOPK))
    weight_codes = place_ends(jax.random.randint(part_keys[2], (REQ, TOPK), 1, 65), jax.random.fold_in(part_keys[2], 1), 1, 64).astype(jnp.int32)
    target_rows = draw_target_rows(jax.random.fold_in(jax.random.fold_in(streams_of[7], part), 71), part)
    norm_gain = jnp.clip(1.0 + 0.1 * jax.random.normal(streams_of[4], (EXPERTS, D), jnp.float32), 0.5, 1.5)
    norm_bias = gaussian(streams_of[5], (EXPERTS, D), 0.5, 3.0, jnp.float32)
    head_weight = draw_head_weight(jax.random.fold_in(streams_of[7], 71), part)
    return dict(hidden_rows=hidden_rows, expert_ids=expert_ids, weight_codes=weight_codes, target_rows=target_rows, norm_gain=norm_gain, norm_bias=norm_bias, head_weight=head_weight)


def layer_norm(source, gain, bias):
    values = source.astype(jnp.float32)
    center = values - lax.optimization_barrier(jnp.mean(values, axis=-1, keepdims=True))
    spread = lax.optimization_barrier(jnp.mean(center * center, axis=-1, keepdims=True))
    return (center * jax.lax.rsqrt(spread + 1e-05) * gain + bias).astype(jnp.bfloat16)

def reference(hidden_rows, expert_ids, weight_codes, target_rows, norm_gain, norm_bias, head_weight):
    code_total = lax.optimization_barrier(jnp.sum(weight_codes, axis=1))
    weights = weight_codes.astype(jnp.float32) / code_total[:, None].astype(jnp.float32)
    limit = MOST * (REQ // REQ_DEV)
    places = jnp.arange(TOPK, dtype=jnp.int32)
    scores = jnp.zeros((REQ, TOPK, VOCAB), jnp.float32)
    for expert in range(EXPERTS):
        matches = expert_ids == expert
        chosen = jnp.any(matches, axis=1)
        order = jnp.argsort(jnp.where(chosen, 0, 1).astype(jnp.int32), stable=True)[:limit].astype(jnp.int32)
        count = jnp.sum(chosen.astype(jnp.int32))
        column = lax.optimization_barrier(jnp.sum(jnp.where(matches, places[None, :], 0), axis=1)).astype(jnp.int32)
        kept = jnp.arange(limit, dtype=jnp.int32) < count
        target = jnp.where(kept, order, REQ).astype(jnp.int32)
        normed = layer_norm(hidden_rows[order], norm_gain[expert], norm_bias[expert])
        logits = jnp.dot(normed, head_weight[:, expert * VOCAB:(expert + 1) * VOCAB], preferred_element_type=jnp.float32)
        top = lax.optimization_barrier(jnp.max(logits, axis=1))
        total = lax.optimization_barrier(jnp.sum(jnp.exp(logits - top[:, None]), axis=1))
        weight = weights[order, column[order]]
        score = logits - top[:, None] - jnp.log(total)[:, None] + jnp.log(weight)[:, None]
        scores = scores.at[target, column[order]].set(score, mode='drop')
    peak = lax.optimization_barrier(jnp.max(scores, axis=1))
    mixed = peak + jnp.log(lax.optimization_barrier(jnp.sum(jnp.exp(scores - peak[:, None, :]), axis=1)))
    owner_start = jnp.arange(REQ, dtype=jnp.int32) // REQ_DEV * REQ_DEV
    global_rows = (owner_start + target_rows).astype(jnp.int32)
    return jnp.zeros((REQ, VOCAB), jnp.float32).at[global_rows].set(mixed)
```

```python
import functools

import jax
import jax.numpy as jnp
from jax import lax
from jax.experimental import pallas as pl
from jax.experimental.pallas import tpu as pltpu
from jax.sharding import PartitionSpec as P

MOST = 2
LANES = 128
NEGATIVE = -1e30
CHUNK = 512
GROUP = 1024
SLOTS = 12
STEPS = 32000.0
VMEM_BYTES = 60 * 2**20


def kernel(
    experts, ids, codes, target, hidden, gain, bias, weight, out,
    hidden_v, gain_v, bias_v, rows3, gain3, bias3, picked, arrived, wide, lhs, held,
    natural, coded, quant, landed, stats, stat_out, stat_in, offsets,
    small_sem, held_sem, row_send, row_recv, data_send, data_recv, stat_send, stat_recv,
):
    clusters = lax.axis_size("cluster")
    tensors = lax.axis_size("tensor")
    sources = clusters * tensors
    per = sources // experts
    me = lax.axis_index("cluster") * tensors + lax.axis_index("tensor")
    mine = me // per
    block, topk = ids.shape
    depth = hidden.shape[1]
    width = weight.shape[1]
    groups = width // GROUP
    chunks = width // CHUNK
    parts = GROUP // CHUNK
    slots = held.shape[0]
    tall = GROUP // LANES
    rows = MOST * sources

    def device(p):
        return {"cluster": p // tensors, "tensor": lax.rem(p, tensors)}

    def other(i):
        return lax.rem(me + i, sources)

    def fetch(c, slot):
        return pltpu.make_async_copy(
            weight.at[:, pl.ds(pl.multiple_of(c * CHUNK, CHUNK), CHUNK)],
            held.at[slot],
            held_sem.at[slot],
        )

    small = [
        pltpu.make_async_copy(src, dst, small_sem.at[i])
        for i, (src, dst) in enumerate(((hidden, hidden_v), (gain, gain_v), (bias, bias_v)))
    ]
    for copy in small:
        copy.start()
    for c in range(slots):
        fetch(c, c).start()

    barrier = pltpu.get_barrier_semaphore()

    @pl.loop(1, sources)
    def _(i):
        pl.semaphore_signal(
            barrier, inc=1, device_id=device(other(i)), device_id_type=pl.DeviceIdType.MESH
        )

    for copy in small:
        copy.wait()
    values = hidden_v[...].astype(jnp.float32)
    center = values - jnp.mean(values, axis=-1, keepdims=True)
    spread = jnp.mean(center * center, axis=-1, keepdims=True)
    scaled = center * lax.rsqrt(spread + 1e-05)
    for k in range(depth // LANES):
        part = slice(k * LANES, (k + 1) * LANES)
        rows3[:, k, :] = scaled[:, part]
        gain3[:, k, :] = gain_v[:, part]
        bias3[:, k, :] = bias_v[:, part]

    def names(r, e):
        hit = ids[r, 0] == e
        for k in range(1, topk):
            hit = hit | (ids[r, k] == e)
        return hit.astype(jnp.int32)

    for e in range(experts):
        for m in range(MOST):
            row, rank = jnp.int32(0), jnp.int32(0)
            for r in range(block):
                hit = names(r, e)
                row = row + jnp.where(rank == m, hit * r, 0)
                rank = rank + hit
            picked[e, m] = (rows3[row] * gain3[e] + bias3[e]).astype(jnp.bfloat16)

    pl.semaphore_wait(barrier, sources - 1)

    @pl.loop(1, sources)
    def _(i):
        p = other(i)
        pltpu.make_async_remote_copy(
            picked.at[p // per], arrived.at[me], row_send, row_recv,
            device_id=device(p), device_id_type=pl.DeviceIdType.MESH,
        ).start()

    pltpu.make_async_copy(picked.at[mine], arrived.at[me], row_recv).start()
    lane = lax.broadcasted_iota(jnp.int32, (rows, LANES), 1)
    stats[0] = jnp.full((rows, LANES), NEGATIVE, jnp.float32)
    for q in range(1, 4):
        stats[q] = jnp.zeros((rows, LANES), jnp.float32)
    for q in range(4, 8):
        stat_out[:, q, :] = jnp.zeros((rows, LANES), jnp.float32)
    pltpu.make_async_copy(arrived, arrived, row_recv).wait()
    wide[...] = arrived[...].astype(jnp.float32).reshape(wide.shape)
    for k in range(depth // LANES):
        lhs[:, k * LANES:(k + 1) * LANES] = wide[:, k, :].astype(jnp.bfloat16)

    def wait_send(g):
        gone = quant.at[g, pl.ds(0, sources - 1)]
        pltpu.make_async_copy(gone, gone, data_send.at[g]).wait()

    def wait_recv(g):
        pltpu.make_async_copy(landed.at[g], landed.at[g], data_recv.at[g]).wait()

    @pl.loop(0, groups)
    def _(g):
        for h in range(parts):
            c = g * parts + h
            slot = lax.rem(c, slots)
            fetch(c, slot).wait()
            natural[:, h * CHUNK:(h + 1) * CHUNK] = jnp.dot(
                lhs[...], held[slot], preferred_element_type=jnp.float32
            )

            @pl.when(c + slots < chunks)
            def _():
                fetch(c + slots, slot).start()

        pieces = [natural[:, j * LANES:(j + 1) * LANES] for j in range(tall)]
        top = jnp.max(functools.reduce(jnp.maximum, pieces), axis=1, keepdims=True)
        low = jnp.min(functools.reduce(jnp.minimum, pieces), axis=1, keepdims=True)
        middle = 0.5 * top + 0.5 * low
        half = jnp.maximum(top - middle, 1e-20)
        inverse = STEPS / half
        total = jnp.zeros((rows, LANES), jnp.float32)
        for j, piece in enumerate(pieces):
            coded[:, j, :] = jnp.round((piece - middle) * inverse)
            total = total + jnp.exp(piece - top)
        total = jnp.sum(total, axis=1, keepdims=True)
        quant[g] = coded[...].reshape(sources, MOST * tall, LANES).astype(jnp.int32).astype(jnp.int16)
        for q, value in enumerate((top, total, middle, half / STEPS)):
            stats[q] = jnp.where(lane == g, value, stats[q])

        @pl.loop(1, sources)
        def _(i):
            p = other(i)
            pltpu.make_async_remote_copy(
                quant.at[g, p], landed.at[g, me], data_send.at[g], data_recv.at[g],
                device_id=device(p), device_id_type=pl.DeviceIdType.MESH,
            ).start()

        pltpu.make_async_copy(quant.at[g, me], landed.at[g, me], data_recv.at[g]).start()

    for q in range(4):
        stat_out[:, q, :] = stats[q]

    @pl.loop(1, sources)
    def _(i):
        p = other(i)
        pltpu.make_async_remote_copy(
            stat_out.at[pl.ds(MOST * p, MOST)], stat_in.at[me], stat_send, stat_recv,
            device_id=device(p), device_id_type=pl.DeviceIdType.MESH,
        ).start()

    pltpu.make_async_copy(
        stat_out.at[pl.ds(MOST * me, MOST)], stat_in.at[me], stat_recv
    ).start()
    gone_rows = arrived.at[pl.ds(0, sources - 1)]
    pltpu.make_async_copy(gone_rows, gone_rows, row_send).wait()
    pltpu.make_async_copy(stat_in, stat_in, stat_recv).wait()
    for e in range(experts):
        for m in range(MOST):
            owned = slice(e * per, (e + 1) * per)
            tops = stat_in[owned, m, 0, :]
            highest = jnp.max(tops, keepdims=True)
            whole = jnp.sum(stat_in[owned, m, 1, :] * jnp.exp(tops - highest), keepdims=True)
            offsets[e * MOST + m] = (stat_in[owned, m, 2, :] - highest) - jnp.log(whole)

    @pl.loop(0, groups)
    def _(g):
        wait_recv(g)
        wait_send(g)

    for t in range(block):
        r = jnp.int32(0)
        for other_row in range(block):
            r = jnp.where(target[other_row] == t, other_row, r)
        code_total = codes[r, 0]
        for k in range(1, topk):
            code_total = code_total + codes[r, k]
        code_total = jnp.full((1, LANES), code_total, jnp.int32).astype(jnp.float32)
        named = []
        for k in range(topk):
            e = ids[r, k]
            m = jnp.int32(0)
            for other_row in range(block):
                m = m + jnp.where(other_row < r, names(other_row, e), 0)
            m = jnp.minimum(m, MOST - 1)
            share = jnp.full((1, LANES), codes[r, k], jnp.int32).astype(jnp.float32) / code_total
            named.append((e, m, jnp.log(share)))

        @pl.loop(0, per)
        def _(j):
            loaded = []
            for e, m, log_share in named:
                step = stat_in[e * per + j, m][3:4]
                offset = offsets[e * MOST + m, pl.ds(j, 1)] + log_share
                loaded.append((e * per + j, m, step, offset))
            for g in range(groups):
                scores = []
                for source, m, step, offset in loaded:
                    tile = landed[g, source].astype(jnp.int32).astype(jnp.float32)
                    tile = jnp.where(m == 0, tile[:tall], tile[tall:])
                    scores.append(tile * step[:, g:g + 1] + offset[:, g:g + 1])
                peak = functools.reduce(jnp.maximum, scores)
                summed = sum(jnp.exp(score - peak) for score in scores)
                place = pl.multiple_of((j * groups + g) * tall, tall)
                out[pl.ds(place, tall), t, :] = peak + jnp.log(summed)

    gone_stats = stat_out.at[pl.ds(0, MOST * (sources - 1))]
    pltpu.make_async_copy(gone_stats, gone_stats, stat_send).wait()


def local(hidden_rows, expert_ids, weight_codes, target_rows, norm_gain, norm_bias, head_weight):
    sources = lax.axis_size("cluster") * lax.axis_size("tensor")
    experts, depth = norm_gain.shape
    block = hidden_rows.shape[0]
    width = head_weight.shape[1]
    per = sources // experts
    rows = MOST * sources
    groups, chunks = width // GROUP, width // CHUNK
    tall = GROUP // LANES
    slots = min(SLOTS, chunks)
    high = depth // LANES
    f32, bf16 = jnp.float32, jnp.bfloat16
    scratch = [
        pltpu.VMEM((block, depth), bf16),
        pltpu.VMEM((experts, depth), f32),
        pltpu.VMEM((experts, depth), f32),
        pltpu.VMEM((block, high, LANES), f32),
        pltpu.VMEM((experts, high, LANES), f32),
        pltpu.VMEM((experts, high, LANES), f32),
        pltpu.VMEM((experts, MOST, high, LANES), bf16),
        pltpu.VMEM((sources, MOST, high, LANES), bf16),
        pltpu.VMEM((rows, high, LANES), f32),
        pltpu.VMEM((rows, depth), bf16),
        pltpu.VMEM((slots, depth, CHUNK), bf16),
        pltpu.VMEM((rows, GROUP), f32),
        pltpu.VMEM((rows, tall, LANES), f32),
        pltpu.VMEM((groups, sources, MOST * tall, LANES), jnp.int16),
        pltpu.VMEM((groups, sources, MOST * tall, LANES), jnp.int16),
        pltpu.VMEM((4, rows, LANES), f32),
        pltpu.VMEM((rows, 8, LANES), f32),
        pltpu.VMEM((sources, MOST, 8, LANES), f32),
        pltpu.VMEM((experts * MOST, per, LANES), f32),
        pltpu.SemaphoreType.DMA((3,)),
        pltpu.SemaphoreType.DMA((slots,)),
        pltpu.SemaphoreType.DMA,
        pltpu.SemaphoreType.DMA,
        pltpu.SemaphoreType.DMA((groups,)),
        pltpu.SemaphoreType.DMA((groups,)),
        pltpu.SemaphoreType.DMA,
        pltpu.SemaphoreType.DMA,
    ]
    smem = pl.BlockSpec(memory_space=pltpu.SMEM)
    anywhere = pl.BlockSpec(memory_space=pl.ANY)
    mixed = pl.pallas_call(
        functools.partial(kernel, experts),
        out_shape=jax.ShapeDtypeStruct((per * width // LANES, block, LANES), f32),
        in_specs=[smem] * 3 + [anywhere] * 4,
        out_specs=pl.BlockSpec(memory_space=pltpu.VMEM),
        scratch_shapes=scratch,
        compiler_params=pltpu.CompilerParams(
            collective_id=0, has_side_effects=True, vmem_limit_bytes=VMEM_BYTES
        ),
        cost_estimate=pl.CostEstimate(
            flops=2 * rows * depth * width,
            bytes_accessed=2 * depth * width,
            transcendentals=3 * rows * width,
        ),
    )(expert_ids, weight_codes, target_rows, hidden_rows, norm_gain, norm_bias, head_weight)
    return jnp.transpose(mixed, (1, 0, 2)).reshape(block, per * width)


def solution(mesh):
    rows = P(("parts", "cluster", "tensor"), None)
    placed = (
        rows,
        rows,
        rows,
        P(("parts", "cluster", "tensor")),
        P(),
        P(),
        P(None, ("cluster", "tensor")),
    )
    return jax.shard_map(
        local, mesh=mesh, in_specs=placed, out_specs=rows, check_vma=False
    )
```

```python
import functools

import jax
import jax.numpy as jnp
from jax import lax
from jax.experimental import pallas as pl
from jax.experimental.pallas import tpu as pltpu
from jax.sharding import PartitionSpec as P

MOST = 2
LANES = 128
NEGATIVE = -1e30
CHUNK = 512
GROUP = 1024
SLOTS = 12
EARLY = 4
STEPS = 32000.0
VMEM_BYTES = 60 * 2**20


def kernel(
    experts, ids, codes, target, hidden, gain, bias, weight, out,
    hidden_v, gain_v, bias_v, rows3, gain3, bias3, picked, arrived, wide, lhs, held,
    natural, coded, quant, landed, stats, stat_out, stat_in, offsets,
    small_sem, held_sem, row_send, row_recv, pass_send, pass_recv, data_send, data_recv, stat_send, stat_recv,
):
    clusters = lax.axis_size("cluster")
    tensors = lax.axis_size("tensor")
    sources = clusters * tensors
    per = sources // experts
    me = lax.axis_index("cluster") * tensors + lax.axis_index("tensor")
    mine = me // per
    topk, block = ids.shape
    spot = lax.rem(me, per)
    depth = hidden.shape[1]
    width = weight.shape[1]
    groups = width // GROUP
    chunks = width // CHUNK
    parts = GROUP // CHUNK
    slots = held.shape[0]
    tall = GROUP // LANES
    rows = MOST * sources

    def device(p):
        return {"cluster": p // tensors, "tensor": lax.rem(p, tensors)}

    def other(i):
        return lax.rem(me + i, sources)

    def fetch(c, slot):
        return pltpu.make_async_copy(
            weight.at[:, pl.ds(pl.multiple_of(c * CHUNK, CHUNK), CHUNK)],
            held.at[slot],
            held_sem.at[slot],
        )

    small = [
        pltpu.make_async_copy(src, dst, small_sem.at[i])
        for i, (src, dst) in enumerate(((hidden, hidden_v), (gain, gain_v), (bias, bias_v)))
    ]
    for copy in small:
        copy.start()
    early = min(EARLY, slots)
    for c in range(early):
        fetch(c, c).start()

    barrier = pltpu.get_barrier_semaphore()

    @pl.loop(1, sources)
    def _(i):
        pl.semaphore_signal(
            barrier, inc=1, device_id=device(other(i)), device_id_type=pl.DeviceIdType.MESH
        )

    for copy in small:
        copy.wait()
    values = hidden_v[...].astype(jnp.float32)
    center = values - jnp.mean(values, axis=-1, keepdims=True)
    spread = jnp.mean(center * center, axis=-1, keepdims=True)
    scaled = center * lax.rsqrt(spread + 1e-05)
    for k in range(depth // LANES):
        part = slice(k * LANES, (k + 1) * LANES)
        rows3[:, k, :] = scaled[:, part]
        gain3[:, k, :] = gain_v[:, part]
        bias3[:, k, :] = bias_v[:, part]

    def names(r, e):
        hit = ids[0, r] == e
        for k in range(1, topk):
            hit = hit | (ids[k, r] == e)
        return hit.astype(jnp.int32)

    for e in range(experts):
        for m in range(MOST):
            row, rank = jnp.int32(0), jnp.int32(0)
            for r in range(block):
                hit = names(r, e)
                row = row + jnp.where(rank == m, hit * r, 0)
                rank = rank + hit
            picked[e, m] = (rows3[row] * gain3[e] + bias3[e]).astype(jnp.bfloat16)

    pl.semaphore_wait(barrier, sources - 1)

    for k in range(1, experts):
        e = lax.rem(mine + k, experts)
        pltpu.make_async_remote_copy(
            picked.at[e], arrived.at[me], row_send, row_recv.at[mine],
            device_id=device(e * per + spot), device_id_type=pl.DeviceIdType.MESH,
        ).start()

    own_rows = pltpu.make_async_copy(picked.at[mine], arrived.at[me], row_recv.at[mine])
    own_rows.start()
    for k in range(experts):
        e = lax.rem(mine - k + experts, experts)
        held_rows = arrived.at[e * per + spot]
        if k:
            pltpu.make_async_copy(held_rows, held_rows, row_recv.at[e]).wait()

        @pl.loop(1, per)
        def _(i):
            pltpu.make_async_remote_copy(
                held_rows if k else picked.at[mine], held_rows, pass_send, pass_recv,
                device_id=device(mine * per + lax.rem(spot + i, per)),
                device_id_type=pl.DeviceIdType.MESH,
            ).start()

    own_rows.wait()
    lane = lax.broadcasted_iota(jnp.int32, (rows, LANES), 1)
    stats[0] = jnp.full((rows, LANES), NEGATIVE, jnp.float32)
    for q in range(1, 4):
        stats[q] = jnp.zeros((rows, LANES), jnp.float32)
    for q in range(4, 8):
        stat_out[:, q, :] = jnp.zeros((rows, LANES), jnp.float32)
    passed = arrived.at[pl.ds(0, sources - experts)]
    pltpu.make_async_copy(passed, passed, pass_recv).wait()
    for c in range(early, slots):
        fetch(c, c).start()
    wide[...] = arrived[...].astype(jnp.float32).reshape(wide.shape)
    for k in range(depth // LANES):
        lhs[:, k * LANES:(k + 1) * LANES] = wide[:, k, :].astype(jnp.bfloat16)

    def wait_send(g):
        gone = quant.at[g, pl.ds(0, sources - 1)]
        pltpu.make_async_copy(gone, gone, data_send.at[g]).wait()

    def wait_recv(g):
        pltpu.make_async_copy(landed.at[g], landed.at[g], data_recv.at[g]).wait()

    @pl.loop(0, groups)
    def _(g):
        for h in range(parts):
            c = g * parts + h
            slot = lax.rem(c, slots)
            fetch(c, slot).wait()
            natural[:, h * CHUNK:(h + 1) * CHUNK] = jnp.dot(
                lhs[...], held[slot], preferred_element_type=jnp.float32
            )

            @pl.when(c + slots < chunks)
            def _():
                fetch(c + slots, slot).start()

        pieces = [natural[:, j * LANES:(j + 1) * LANES] for j in range(tall)]
        top = jnp.max(functools.reduce(jnp.maximum, pieces), axis=1, keepdims=True)
        low = jnp.min(functools.reduce(jnp.minimum, pieces), axis=1, keepdims=True)
        middle = 0.5 * top + 0.5 * low
        half = jnp.maximum(top - middle, 1e-20)
        inverse = STEPS / half
        total = jnp.zeros((rows, LANES), jnp.float32)
        for j, piece in enumerate(pieces):
            coded[:, j, :] = jnp.round((piece - middle) * inverse)
            total = total + jnp.exp(piece - top)
        total = jnp.sum(total, axis=1, keepdims=True)
        quant[g] = coded[...].reshape(sources, MOST * tall, LANES).astype(jnp.int32).astype(jnp.int16)
        for q, value in enumerate((top, total, middle, half / STEPS)):
            stats[q] = jnp.where(lane == g, value, stats[q])

        @pl.loop(1, sources)
        def _(i):
            p = other(i)
            pltpu.make_async_remote_copy(
                quant.at[g, p], landed.at[g, me], data_send.at[g], data_recv.at[g],
                device_id=device(p), device_id_type=pl.DeviceIdType.MESH,
            ).start()

        pltpu.make_async_copy(quant.at[g, me], landed.at[g, me], data_recv.at[g]).start()

    for q in range(4):
        stat_out[:, q, :] = stats[q]

    @pl.loop(1, sources)
    def _(i):
        p = other(i)
        pltpu.make_async_remote_copy(
            stat_out.at[pl.ds(MOST * p, MOST)], stat_in.at[me], stat_send, stat_recv,
            device_id=device(p), device_id_type=pl.DeviceIdType.MESH,
        ).start()

    pltpu.make_async_copy(
        stat_out.at[pl.ds(MOST * me, MOST)], stat_in.at[me], stat_recv
    ).start()
    gone_rows = arrived.at[pl.ds(0, experts - 1)]
    pltpu.make_async_copy(gone_rows, gone_rows, row_send).wait()
    pltpu.make_async_copy(passed, passed, pass_send).wait()
    pltpu.make_async_copy(stat_in, stat_in, stat_recv).wait()
    for e in range(experts):
        for m in range(MOST):
            owned = slice(e * per, (e + 1) * per)
            tops = stat_in[owned, m, 0, :]
            highest = jnp.max(tops, keepdims=True)
            whole = jnp.sum(stat_in[owned, m, 1, :] * jnp.exp(tops - highest), keepdims=True)
            offsets[e * MOST + m] = (stat_in[owned, m, 2, :] - highest) - jnp.log(whole)

    @pl.loop(0, groups)
    def _(g):
        wait_recv(g)
        wait_send(g)

    for t in range(block):
        r = jnp.int32(0)
        for other_row in range(block):
            r = jnp.where(target[other_row] == t, other_row, r)
        code_total = codes[0, r]
        for k in range(1, topk):
            code_total = code_total + codes[k, r]
        code_total = jnp.full((1, LANES), code_total, jnp.int32).astype(jnp.float32)
        named = []
        for k in range(topk):
            e = ids[k, r]
            m = jnp.int32(0)
            for other_row in range(block):
                m = m + jnp.where(other_row < r, names(other_row, e), 0)
            m = jnp.minimum(m, MOST - 1)
            share = jnp.full((1, LANES), codes[k, r], jnp.int32).astype(jnp.float32) / code_total
            named.append((e, m, jnp.log(share)))

        @pl.loop(0, per)
        def _(j):
            loaded = []
            for e, m, log_share in named:
                step = stat_in[e * per + j, m][3:4]
                offset = offsets[e * MOST + m, pl.ds(j, 1)] + log_share
                loaded.append((e * per + j, m, step, offset))
            for g in range(groups):
                scores = []
                for source, m, step, offset in loaded:
                    tile = landed[g, source].astype(jnp.int32).astype(jnp.float32)
                    tile = jnp.where(m == 0, tile[:tall], tile[tall:])
                    scores.append(tile * step[:, g:g + 1] + offset[:, g:g + 1])
                first, second = scores
                peak = jnp.maximum(first, second)
                summed = 1.0 + jnp.exp(jnp.minimum(first, second) - peak)
                place = pl.multiple_of((j * groups + g) * tall, tall)
                out[pl.ds(place, tall), t, :] = peak + jnp.log(summed)

    gone_stats = stat_out.at[pl.ds(0, MOST * (sources - 1))]
    pltpu.make_async_copy(gone_stats, gone_stats, stat_send).wait()


def local(hidden_rows, expert_ids, weight_codes, target_rows, norm_gain, norm_bias, head_weight):
    sources = lax.axis_size("cluster") * lax.axis_size("tensor")
    experts, depth = norm_gain.shape
    block = hidden_rows.shape[0]
    width = head_weight.shape[1]
    per = sources // experts
    rows = MOST * sources
    groups, chunks = width // GROUP, width // CHUNK
    tall = GROUP // LANES
    slots = min(SLOTS, chunks)
    high = depth // LANES
    f32, bf16 = jnp.float32, jnp.bfloat16
    scratch = [
        pltpu.VMEM((block, depth), bf16),
        pltpu.VMEM((experts, depth), f32),
        pltpu.VMEM((experts, depth), f32),
        pltpu.VMEM((block, high, LANES), f32),
        pltpu.VMEM((experts, high, LANES), f32),
        pltpu.VMEM((experts, high, LANES), f32),
        pltpu.VMEM((experts, MOST, high, LANES), bf16),
        pltpu.VMEM((sources, MOST, high, LANES), bf16),
        pltpu.VMEM((rows, high, LANES), f32),
        pltpu.VMEM((rows, depth), bf16),
        pltpu.VMEM((slots, depth, CHUNK), bf16),
        pltpu.VMEM((rows, GROUP), f32),
        pltpu.VMEM((rows, tall, LANES), f32),
        pltpu.VMEM((groups, sources, MOST * tall, LANES), jnp.int16),
        pltpu.VMEM((groups, sources, MOST * tall, LANES), jnp.int16),
        pltpu.VMEM((4, rows, LANES), f32),
        pltpu.VMEM((rows, 8, LANES), f32),
        pltpu.VMEM((sources, MOST, 8, LANES), f32),
        pltpu.VMEM((experts * MOST, per, LANES), f32),
        pltpu.SemaphoreType.DMA((3,)),
        pltpu.SemaphoreType.DMA((slots,)),
        pltpu.SemaphoreType.DMA,
        pltpu.SemaphoreType.DMA((experts,)),
        pltpu.SemaphoreType.DMA,
        pltpu.SemaphoreType.DMA,
        pltpu.SemaphoreType.DMA((groups,)),
        pltpu.SemaphoreType.DMA((groups,)),
        pltpu.SemaphoreType.DMA,
        pltpu.SemaphoreType.DMA,
    ]
    smem = pl.BlockSpec(memory_space=pltpu.SMEM)
    anywhere = pl.BlockSpec(memory_space=pl.ANY)
    mixed = pl.pallas_call(
        functools.partial(kernel, experts),
        out_shape=jax.ShapeDtypeStruct((per * width // LANES, block, LANES), f32),
        in_specs=[smem] * 3 + [anywhere] * 4,
        out_specs=pl.BlockSpec(memory_space=pltpu.VMEM),
        scratch_shapes=scratch,
        compiler_params=pltpu.CompilerParams(
            collective_id=0, has_side_effects=True, vmem_limit_bytes=VMEM_BYTES
        ),
        cost_estimate=pl.CostEstimate(
            flops=2 * rows * depth * width,
            bytes_accessed=2 * depth * width,
            transcendentals=3 * rows * width,
        ),
    )(expert_ids.T, weight_codes.T, target_rows, hidden_rows, norm_gain, norm_bias, head_weight)
    return jnp.transpose(mixed, (1, 0, 2)).reshape(block, per * width)


def solution(mesh):
    rows = P(("parts", "cluster", "tensor"), None)
    placed = (
        rows,
        rows,
        rows,
        P(("parts", "cluster", "tensor")),
        P(),
        P(),
        P(None, ("cluster", "tensor")),
    )
    return jax.shard_map(
        local, mesh=mesh, in_specs=placed, out_specs=rows, check_vma=False
    )
```
